32 devices in a mesh: groups: 2 (over y), acq: 4 (over z), az: 4 (over x, core).
Axes of the slice: x: 2, y: 2, z: 4, core: 2. Of those that a mesh axis runs over, the one named last changes fastest.
Arguments:
- slc: bfloat16 [2, 8, 512, 4096], P(None, ('groups', 'acq'), 'az'), parts along dimension 1, may hold values from -8 to 8
- pairs: int32 [32, 2], P(('groups', 'acq')), parts along dimension 0, may hold values from 0 to 3, as said below
- position: int32 [8], P(('groups', 'acq')), parts along dimension 0, may hold values from 0 to 3, as said below
- ranges: int32 [32, 2], P(('groups', 'acq')), parts along dimension 0, may hold values from 0 to 512, as said below
Outputs:
- filtered: float32 [2, 32, 64, 128], P(None, ('groups', 'acq'), 'az'), parts along dimension 1
- coherence: float32 [32, 64, 128], P(('groups', 'acq'), 'az'), parts along dimension 0
The draws below stay inside these ranges and needn't reach their ends.
There are 2 independent parts, one for each index of `groups`. The reference program is written for one: setup_inputs(seed, part) draws one part's arguments, and reference() takes and returns one part's arrays. A program takes and returns all parts, laid end to end along the dimension named above; each array names one. Nothing has to cross between parts.
Inputs may be any that keep to these rules, and one draw needn't show every extreme that they name: `pairs`: row p * 4 + j names as reference the acquisition stored at row p of slc; its secondaries are 4 distinct later acquisitions at most 8 later; a slot whose partner would lie past the last acquisition names the reference twice. A permutation: position[t] is the storage row of acquisition t. `ranges`: first <= last; the range is empty, (0, 0), exactly for slots that name the reference twice.
All inputs are finite; a program needn't handle non-finite values.
Results may differ from the reference program's by a relative error of at most 0.0003.
Values may be sent and summed in bfloat16 or wider, within the bound.
A program may use at most 64 MiB of HBM per device.

```python
import math
import jax
import jax.numpy as jnp
from jax import lax

RW = 4096
LA = 8
LR = 32
PATCH = 32
PPA = 4
SPAN = 8
ACQ = 4
AZ = 512
MLA = 64
MLR = 128


def pair_table(key):
    base_key = jax.random.fold_in(key, 7001)
    key_order, key_pick, key_first, key_last = jax.random.split(base_key, 4)
    position = jax.random.permutation(key_order, ACQ).astype(jnp.int32)
    time_of = jnp.argsort(position).astype(jnp.int32)
    scores = jax.random.randint(key_pick, (ACQ, SPAN), 0, 1 << 16) * SPAN + jnp.arange(SPAN, dtype=jnp.int32)[None, :]
    offsets = (jnp.argsort(scores, axis=1)[:, :PPA] + 1).astype(jnp.int32)
    reference_time = jnp.repeat(time_of, PPA)
    partner_time = reference_time + offsets[time_of].reshape(-1)
    alive_slot = partner_time < ACQ
    secondary = jnp.where(alive_slot, partner_time, reference_time).astype(jnp.int32)
    quarter = AZ // 4
    first_line = jnp.clip(jax.random.randint(key_first, (ACQ * PPA,), -quarter, quarter), 0, AZ)
    last_line = jnp.clip(AZ - jax.random.randint(key_last, (ACQ * PPA,), -quarter, quarter), 0, AZ)
    first_line = jnp.where(alive_slot, first_line, 0).astype(jnp.int32)
    last_line = jnp.where(alive_slot, last_line, 0).astype(jnp.int32)
    pair_rows = jnp.stack([reference_time, secondary], axis=1).astype(jnp.int32)
    range_rows = jnp.stack([first_line, last_line], axis=1).astype(jnp.int32)
    return (pair_rows, position, range_rows)


def draw_pairs(key, part):
    return pair_table(key)[0]


def draw_position(key, part):
    return pair_table(key)[1]


def draw_ranges(key, part):
    return pair_table(key)[2]


def draw_slc(key, part):
    key_scene, key_each = jax.random.split(jax.random.fold_in(key, 3301), 2)
    scene_field = jax.random.normal(key_scene, (2, AZ, RW), jnp.float32)
    line_frac = (jnp.arange(AZ, dtype=jnp.float32) / AZ)[:, None]
    column_frac = (jnp.arange(RW, dtype=jnp.float32) / RW)[None, :]

    def one_acquisition(acq_number):
        key_noise, key_slope, key_mix = jax.random.split(jax.random.fold_in(key_each, acq_number), 3)
        speckle = jax.random.normal(key_noise, (2, AZ, RW), jnp.float32)
        slopes = jax.random.uniform(key_slope, (3,), jnp.float32, -6.0, 6.0)
        mixing = jax.random.uniform(key_mix, (), jnp.float32, 0.5, 0.95)
        remainder = jnp.sqrt(1.0 - mixing * mixing)
        base_re = mixing * scene_field[0] + remainder * speckle[0]
        base_im = mixing * scene_field[1] + remainder * speckle[1]
        phase_screen = 2.0 * math.pi * (slopes[0] * line_frac + slopes[1] * column_frac) + slopes[2]
        cosine = jnp.cos(phase_screen)
        sine = jnp.sin(phase_screen)
        rotated = jnp.stack([base_re * cosine - base_im * sine, base_re * sine + base_im * cosine])
        return jnp.clip(rotated, -8.0, 8.0).astype(jnp.bfloat16)
    stacked = lax.map(one_acquisition, jnp.arange(ACQ, dtype=jnp.int32))
    return jnp.moveaxis(stacked, 0, 1)


def setup_inputs(seed: int = 0, part: int = 0) -> dict:
    keys = jax.random.split(jax.random.key(seed), 5)
    part_splits = jax.random.split(jax.random.fold_in(keys[4], part), 5)
    return {
        "slc": draw_slc(jax.random.fold_in(jax.random.fold_in(keys[4], part), 71), part),
        "pairs": draw_pairs(jax.random.fold_in(jax.random.fold_in(keys[4], part), 71), part),
        "position": draw_position(jax.random.fold_in(jax.random.fold_in(keys[4], part), 71), part),
        "ranges": draw_ranges(jax.random.fold_in(jax.random.fold_in(keys[4], part), 71), part),
    }


def hann_window(length_cells):
    steps = (jnp.arange(length_cells, dtype=jnp.float32) + 0.5) * (math.pi / length_cells)
    return jnp.sin(steps) ** 2

def goldstein(field_re, field_im):
    half_patch = PATCH // 2
    padded_re = jnp.pad(field_re, ((half_patch, half_patch), (0, 0)))
    padded_im = jnp.pad(field_im, ((half_patch, half_patch), (0, 0)))
    window = hann_window(PATCH)
    taper = window[:, None] * window[None, :]
    corners = [(row_k * half_patch, col_k * half_patch) for row_k in range(MLA // half_patch + 1) for col_k in range(2 * MLR // PATCH - 1)]
    patches = jnp.stack([lax.complex(padded_re[row_at:row_at + PATCH, col_at:col_at + PATCH] * taper, padded_im[row_at:row_at + PATCH, col_at:col_at + PATCH] * taper) for row_at, col_at in corners])
    spectrum = jnp.fft.fft2(patches)
    amplitude = (jnp.real(spectrum) ** 2 + jnp.imag(spectrum) ** 2 + 1e-06) ** 0.25
    response = amplitude / lax.optimization_barrier(jnp.mean(amplitude, axis=(1, 2), keepdims=True))
    restored = jnp.fft.ifft2(response * spectrum)
    summed_re = jnp.zeros_like(padded_re)
    summed_im = jnp.zeros_like(padded_im)
    for number, (row_at, col_at) in enumerate(corners):
        summed_re = summed_re.at[row_at:row_at + PATCH, col_at:col_at + PATCH].add(jnp.real(restored[number]))
        summed_im = summed_im.at[row_at:row_at + PATCH, col_at:col_at + PATCH].add(jnp.imag(restored[number]))
    return (summed_re[half_patch:half_patch + MLA], summed_im[half_patch:half_patch + MLA])

def multilook(values):
    return lax.optimization_barrier(jnp.sum(values.reshape(MLA, LA, MLR, LR), axis=(1, 3))) / (LA * LR)

def reference(slc, pairs, position, ranges):
    ref_rows = position[pairs[:, 0]].astype(jnp.int32)
    sec_rows = position[pairs[:, 1]].astype(jnp.int32)
    line_index = jnp.arange(AZ, dtype=jnp.int32)

    def one_pair(pair_item):
        ref_row, sec_row, first_line, last_line = pair_item
        primary = lax.dynamic_index_in_dim(slc, ref_row, 1, keepdims=False).astype(jnp.float32)
        partner = lax.dynamic_index_in_dim(slc, sec_row, 1, keepdims=False).astype(jnp.float32)
        alive = ((line_index >= first_line) & (line_index < last_line)).astype(jnp.float32)[:, None]
        look_re = multilook((primary[0] * partner[0] + primary[1] * partner[1]) * alive)
        look_im = multilook((primary[1] * partner[0] - primary[0] * partner[1]) * alive)
        look_ref = multilook((primary[0] * primary[0] + primary[1] * primary[1]) * alive)
        look_sec = multilook((partner[0] * partner[0] + partner[1] * partner[1]) * alive)
        denominator = jnp.maximum(jnp.sqrt(look_ref * look_sec), 0.5)
        coherent_re = look_re / denominator
        coherent_im = look_im / denominator
        magnitude = jnp.sqrt(coherent_re * coherent_re + coherent_im * coherent_im)
        filt_re, filt_im = goldstein(coherent_re, coherent_im)
        return (jnp.stack([filt_re, filt_im]), magnitude)
    filtered, coherence = lax.map(one_pair, (ref_rows, sec_rows, ranges[:, 0], ranges[:, 1]))
    return (jnp.moveaxis(filtered, 0, 1), coherence)
```

```python
import functools
import math

import jax
import jax.numpy as jnp
import numpy as np
from jax import lax
from jax.experimental import pallas as pl
from jax.experimental.pallas import tpu as pltpu
from jax.sharding import PartitionSpec as P

LA = 8
LR = 32
PATCH = 32
HALF = PATCH // 2
MESH = pl.DeviceIdType.MESH


def look_table(width, slots):
    looks = width // LR
    table = np.zeros((slots, width, 128), np.float32)
    for j in range(slots):
        table[j, np.arange(width), j * looks + np.arange(width) // LR] = 1.0
    return jnp.asarray(table, jnp.bfloat16)


def split_dot(values, table):
    high = values.astype(jnp.bfloat16)
    low = (values - high.astype(jnp.float32)).astype(jnp.bfloat16)
    return jnp.dot(high, table, preferred_element_type=jnp.float32) + jnp.dot(
        low, table, preferred_element_type=jnp.float32
    )


def cross_kernel(n, slots, chunks, tab, x, table, out, *scratch):
    strips = scratch[:chunks]
    power, ready, landed, own_sem, send_sem, recv_sem, back_send, back_recv = scratch[chunks:]
    me = lax.axis_index("acq")
    lines = x.shape[2]
    width = x.shape[3] // n
    looks = width // LR
    step = lines // chunks
    rows = step // LA
    barrier = pltpu.get_barrier_semaphore()

    def peer(k):
        return lax.rem(me + k, n)

    def greet(k, carry):
        pl.semaphore_signal(barrier, inc=1, device_id={"acq": peer(k)}, device_id_type=MESH)
        return carry

    def strip_copy(c, k):
        return pltpu.make_async_remote_copy(
            src_ref=x.at[:, 0, pl.ds(c * step, step), pl.ds(pl.multiple_of(peer(k) * width, 128), width)],
            dst_ref=strips[c].at[k],
            send_sem=send_sem.at[c, k],
            recv_sem=recv_sem.at[c, k],
            device_id={"acq": peer(k)},
            device_id_type=MESH,
        )

    def own_copy(c):
        return pltpu.make_async_copy(
            x.at[:, 0, pl.ds(c * step, step), pl.ds(pl.multiple_of(me * width, 128), width)],
            strips[c].at[0],
            own_sem.at[c],
        )

    def back_copy(k):
        return pltpu.make_async_remote_copy(
            src_ref=ready.at[k],
            dst_ref=landed.at[me],
            send_sem=back_send.at[k],
            recv_sem=back_recv.at[k],
            device_id={"acq": peer(k)},
            device_id_type=MESH,
        )

    for c in range(chunks):
        own_copy(c).start()
    lax.fori_loop(1, n, greet, 0)
    pl.semaphore_wait(barrier, n - 1)
    for c in range(chunks):
        def send(k, carry, c=c):
            strip_copy(c, k).start()
            return carry
        lax.fori_loop(1, n, send, 0)

    lane_slot = lax.broadcasted_iota(jnp.int32, (step, 128), 1) // looks
    first_line = lax.axis_index("az") * lines
    every_slot = table[0]
    for j in range(1, slots):
        every_slot = every_slot + table[j]

    def slot_of(row):
        return lax.rem(me - row + n, n)

    for c in range(chunks):
        own_copy(c).wait()

        def arrive(k, carry, c=c):
            strip_copy(c, k).wait_recv()
            return carry
        lax.fori_loop(1, n, arrive, 0)
        line = first_line + c * step + lax.broadcasted_iota(jnp.int32, (step, 128), 0)

        def powers(k, carry, c=c):
            re = strips[c][k, 0].astype(jnp.float32)
            im = strips[c][k, 1].astype(jnp.float32)
            power[k] = split_dot(re * re + im * im, every_slot)
            return carry
        lax.fori_loop(0, n, powers, 0)

        def pairs_of(k, carry, c=c, line=line):
            row = peer(k)
            at = slot_of(row)
            ref_re = strips[c][at, 0].astype(jnp.float32)
            ref_im = strips[c][at, 1].astype(jnp.float32)
            sum_re = jnp.zeros((step, 128), jnp.float32)
            sum_im = jnp.zeros((step, 128), jnp.float32)
            sec_power = jnp.zeros((step, 128), jnp.float32)
            alive = jnp.zeros((step, 128), jnp.float32)
            for j in range(slots):
                q = row * slots + j
                other = slot_of(tab[0, q])
                sec_re = strips[c][other, 0].astype(jnp.float32)
                sec_im = strips[c][other, 1].astype(jnp.float32)
                sum_re = sum_re + split_dot(ref_re * sec_re + ref_im * sec_im, table[j])
                sum_im = sum_im + split_dot(ref_im * sec_re - ref_re * sec_im, table[j])
                mine = lane_slot == j
                sec_power = jnp.where(mine, power[other], sec_power)
                alive = jnp.where(mine & (line >= tab[1, q]) & (line < tab[2, q]), 1.0, alive)

            def multilook(values):
                return jnp.sum((values * alive).reshape(rows, LA, 128), axis=1) / (LA * LR)

            look_re = multilook(sum_re)
            look_im = multilook(sum_im)
            denominator = jnp.maximum(jnp.sqrt(multilook(power[at]) * multilook(sec_power)), 0.5)
            coherent_re = look_re / denominator
            coherent_im = look_im / denominator
            ready[k, 0, pl.ds(c * rows, rows)] = coherent_re
            ready[k, 1, pl.ds(c * rows, rows)] = coherent_im
            ready[k, 2, pl.ds(c * rows, rows)] = jnp.sqrt(
                coherent_re * coherent_re + coherent_im * coherent_im
            )
            return carry

        def pairs_and_send(k, carry):
            pairs_of(k, carry)
            back_copy(k).start()
            return carry

        if c < chunks - 1:
            lax.fori_loop(0, n, pairs_of, 0)
        else:
            lax.fori_loop(1, n, pairs_and_send, 0)
            pairs_of(0, 0)

    def finish(k, carry):
        back_copy(k).wait_recv()
        return carry
    lax.fori_loop(1, n, finish, 0)

    lane = lax.broadcasted_iota(jnp.int32, (3, lines // LA, 128), 2) // looks
    total = [jnp.zeros((3, lines // LA, 128), jnp.float32) for _ in range(slots)]
    for d in range(n):
        piece = jnp.where(me == d, ready[0], landed[d])
        for j in range(slots):
            shift = ((d - j) * looks) % 128
            moved = pltpu.roll(piece, shift, 2) if shift else piece
            total[j] = jnp.where(lane == d, moved, total[j])
    for j in range(slots):
        out[:, j] = total[j]

    def drain(k, carry):
        for c in range(chunks):
            strip_copy(c, k).wait_send()
        back_copy(k).wait_send()
        return carry
    lax.fori_loop(1, n, drain, 0)


def coherences(slc, tab, n, slots):
    lines, samples = slc.shape[2:]
    width = samples // n
    chunks = 2
    rows = lines // LA
    return pl.pallas_call(
        functools.partial(cross_kernel, n, slots, chunks),
        out_shape=jax.ShapeDtypeStruct((3, slots, rows, 128), jnp.float32),
        in_specs=[
            pl.BlockSpec(memory_space=pltpu.SMEM),
            pl.BlockSpec(memory_space=pl.ANY),
            pl.BlockSpec(memory_space=pltpu.VMEM),
        ],
        out_specs=pl.BlockSpec(memory_space=pltpu.VMEM),
        scratch_shapes=[pltpu.VMEM((n, 2, lines // chunks, width), jnp.bfloat16)] * chunks
        + [
            pltpu.VMEM((n, lines // chunks, 128), jnp.float32),
            pltpu.VMEM((n, 3, rows, 128), jnp.float32),
            pltpu.VMEM((n, 3, rows, 128), jnp.float32),
            pltpu.SemaphoreType.DMA((chunks,)),
            pltpu.SemaphoreType.DMA((chunks, n)),
            pltpu.SemaphoreType.DMA((chunks, n)),
            pltpu.SemaphoreType.DMA((n,)),
            pltpu.SemaphoreType.DMA((n,)),
        ],
        compiler_params=pltpu.CompilerParams(
            collective_id=0, has_side_effects=True, vmem_limit_bytes=32 * 2**20
        ),
    )(tab, slc, look_table(width, slots))


def goldstein_tables(columns):
    ticks = np.arange(PATCH)
    angle = 2.0 * math.pi / PATCH * ((ticks[:, None] * ticks[None, :]) % PATCH)
    cos, sin = np.cos(angle), np.sin(angle)
    window = np.sin((ticks + 0.5) * (math.pi / PATCH)) ** 2
    left = np.block([[cos, sin], [-sin, cos]]) * np.tile(window, 2)[None, :]
    left_back = np.block([[cos, -sin], [sin, cos]]) / (PATCH * PATCH)
    eye = np.eye(columns // PATCH)
    wide_cos, wide_sin = np.kron(eye, cos), np.kron(eye, sin)
    wide_window = np.tile(window, columns // PATCH)
    forward, backward = [], []
    for offset in (0, HALF):
        keep = np.arange(columns) < (columns - PATCH if offset else columns)
        scale = (wide_window * keep)[:, None]
        into = [np.roll(scale * m, offset, axis=0) for m in (wide_cos, wide_sin)]
        forward.append(np.block([[into[0], -into[1]], [into[1], into[0]]]))
        back = [np.roll(m * keep[None, :], offset, axis=1) for m in (wide_cos, wide_sin)]
        backward.append(np.block([[back[0], back[1]], [-back[1], back[0]]]))
    ones = np.kron(eye, np.ones((PATCH, PATCH))) / (PATCH * PATCH)
    arrays = (left, left_back, np.concatenate(forward, 1), np.concatenate(backward, 0), ones)
    return tuple(jnp.asarray(a, jnp.float32) for a in arrays)


def goldstein_kernel(cells, left, left_back, forward, backward, ones, out):
    dot = functools.partial(
        jnp.dot, precision=lax.Precision.HIGHEST, preferred_element_type=jnp.float32
    )
    slots, extended, columns = cells.shape[1:]
    own = extended - 2 * HALF
    count = own // HALF + 1
    wide = dot(
        jnp.concatenate(
            [cells[0].reshape(slots * extended, columns), cells[1].reshape(slots * extended, columns)],
            axis=1,
        ),
        forward[...],
    )
    pieces = [(s, k, o) for s in range(slots) for k in range(count) for o in range(2)]

    def part(s, k, o, plane):
        row = s * extended + k * HALF
        col = (2 * o + plane) * columns
        return wide[row : row + PATCH, col : col + columns]

    stacked = jnp.concatenate(
        [jnp.concatenate([part(*p, 0) for p in pieces], axis=1),
         jnp.concatenate([part(*p, 1) for p in pieces], axis=1)],
        axis=0,
    )
    spectrum = dot(left[...], stacked)
    spec_re, spec_im = spectrum[:PATCH], spectrum[PATCH:]
    amplitude = jnp.sqrt(jnp.sqrt(spec_re * spec_re + spec_im * spec_im + 1e-06))
    sums = jnp.sum(amplitude, axis=0, keepdims=True)
    sums = jnp.concatenate(
        [sums[:, i * columns : (i + 1) * columns] for i in range(len(pieces))], axis=0
    )
    means = dot(sums, ones[...])
    means = jnp.concatenate([means[i : i + 1] for i in range(len(pieces))], axis=1)
    response = amplitude / means
    restored = dot(
        left_back[...], jnp.concatenate([response * spec_re, response * spec_im], axis=0)
    )

    def taken(s, k, o, plane, low):
        row = plane * PATCH + low
        col = pieces.index((s, k, o)) * columns
        return restored[row : row + HALF, col : col + columns]

    summed = jnp.concatenate(
        [
            jnp.concatenate(
                [
                    taken(s, r, o, plane, HALF) + taken(s, r + 1, o, plane, 0)
                    for o in range(2)
                    for plane in range(2)
                ],
                axis=1,
            )
            for s in range(slots)
            for r in range(own // HALF)
        ],
        axis=0,
    )
    result = dot(summed, backward[...])
    for plane in range(2):
        out[plane] = result[:, plane * columns : (plane + 1) * columns].reshape(slots, own, columns)


def with_halo(cells, axis, dim, width):
    count = lax.axis_size(axis)
    head = lax.slice_in_dim(cells, 0, width, axis=dim)
    tail = lax.slice_in_dim(cells, cells.shape[dim] - width, cells.shape[dim], axis=dim)
    return jnp.concatenate(
        [
            lax.ppermute(tail, axis, [(i, i + 1) for i in range(count - 1)]),
            cells,
            lax.ppermute(head, axis, [(i + 1, i) for i in range(count - 1)]),
        ],
        axis=dim,
    )


def local(slc, pairs, position, ranges):
    n = lax.axis_size("acq")
    slots = pairs.shape[0]
    mine = jnp.concatenate([pairs[:, 1], ranges[:, 0], ranges[:, 1], position])
    every = lax.all_gather(mine, "acq", axis=0, tiled=False)
    sec_time = every[:, :slots].reshape(-1)
    time_index = jnp.arange(n, dtype=jnp.int32)
    sec_row = jnp.sum(
        jnp.where(sec_time[:, None] == time_index[None, :], every[:, 3 * slots][None, :], 0), axis=1
    )
    tab = jnp.stack(
        [sec_row, every[:, slots : 2 * slots].reshape(-1), every[:, 2 * slots : 3 * slots].reshape(-1)]
    )
    planes = coherences(slc, tab, n, slots)
    extended = with_halo(planes[:2], "az", 2, HALF)
    filtered = pl.pallas_call(
        goldstein_kernel,
        out_shape=jax.ShapeDtypeStruct((2,) + planes.shape[1:], jnp.float32),
        compiler_params=pltpu.CompilerParams(vmem_limit_bytes=32 * 2**20),
    )(extended, *goldstein_tables(planes.shape[-1]))
    return (filtered, planes[2])


def solution(mesh):
    return jax.shard_map(
        local,
        mesh=mesh,
        in_specs=(
            P(None, ("groups", "acq"), "az", None),
            P(("groups", "acq"), None),
            P(("groups", "acq")),
            P(("groups", "acq"), None),
        ),
        out_specs=(P(None, ("groups", "acq"), "az", None), P(("groups", "acq"), "az", None)),
        check_vma=False,
    )
```

```python
import functools
import math

import jax
import jax.numpy as jnp
import numpy as np
from jax import lax
from jax.experimental import pallas as pl
from jax.experimental.pallas import tpu as pltpu
from jax.sharding import PartitionSpec as P

LA = 8
LR = 32
PATCH = 32
HALF = PATCH // 2
MESH = pl.DeviceIdType.MESH


def look_table(width, slots):
    looks = width // LR
    table = np.zeros((slots, width, 128), np.float32)
    for j in range(slots):
        table[j, np.arange(width), j * looks + np.arange(width) // LR] = 1.0
    return jnp.asarray(table, jnp.bfloat16)


def split_dot(values, table):
    high = values.astype(jnp.bfloat16)
    low = (values - high.astype(jnp.float32)).astype(jnp.bfloat16)
    return jnp.dot(high, table, preferred_element_type=jnp.float32) + jnp.dot(
        low, table, preferred_element_type=jnp.float32
    )


def whole_kernel(n, slots, chunks, pairs, position, ranges, x, table_hbm, *rest):
    tables_hbm, (filtered, magnitude), scratch = rest[:5], rest[5:7], rest[7:]
    strips, scratch = scratch[:chunks], scratch[chunks:]
    table, tables, scratch = scratch[0], scratch[1:6], scratch[6:]
    mine, gathered, tab, power, ready, landed, cells, halo, scratch = *scratch[:8], scratch[8:]
    own_sem, send_sem, recv_sem, back_send, back_recv, tab_send, tab_recv, table_sem, halo_send, halo_recv = scratch
    me = lax.axis_index("acq")
    az = lax.axis_index("az")
    az_count = lax.axis_size("az")
    lines = x.shape[2]
    width = x.shape[3] // n
    looks = width // LR
    step = lines // chunks
    rows = step // LA
    own = lines // LA
    barrier = pltpu.get_barrier_semaphore()

    def peer(k):
        return lax.rem(me + k, n)

    def greet(k, carry):
        pl.semaphore_signal(barrier, inc=1, device_id={"acq": peer(k)}, device_id_type=MESH)
        return carry

    def strip_copy(c, k):
        return pltpu.make_async_remote_copy(
            src_ref=x.at[:, 0, pl.ds(c * step, step), pl.ds(pl.multiple_of(peer(k) * width, 128), width)],
            dst_ref=strips[c].at[k],
            send_sem=send_sem.at[c, k],
            recv_sem=recv_sem.at[c, k],
            device_id={"acq": peer(k)},
            device_id_type=MESH,
        )

    def own_copy(c):
        return pltpu.make_async_copy(
            x.at[:, 0, pl.ds(c * step, step), pl.ds(pl.multiple_of(me * width, 128), width)],
            strips[c].at[0],
            own_sem.at[c],
        )

    def tab_copy(k):
        return pltpu.make_async_remote_copy(
            src_ref=mine,
            dst_ref=gathered.at[me],
            send_sem=tab_send.at[k],
            recv_sem=tab_recv.at[k],
            device_id={"acq": peer(k)},
            device_id_type=MESH,
        )

    def back_copy(k):
        return pltpu.make_async_remote_copy(
            src_ref=ready.at[k],
            dst_ref=landed.at[me],
            send_sem=back_send.at[k],
            recv_sem=back_recv.at[k],
            device_id={"acq": peer(k)},
            device_id_type=MESH,
        )

    def halo_copy(side):
        return pltpu.make_async_remote_copy(
            src_ref=cells.at[:, :, pl.ds(0 if side == 0 else own - HALF, HALF)],
            dst_ref=halo.at[side],
            send_sem=halo_send.at[side],
            recv_sem=halo_recv.at[side],
            device_id={"az": az + (2 * side - 1)},
            device_id_type=MESH,
        )

    has = (az > 0, az < az_count - 1)
    mine[...] = jnp.zeros_like(mine)
    mine[0:2, 0:slots] = pairs[...]
    mine[2:4, 0:slots] = ranges[...]
    mine[4:5, 0:1] = position[...]
    for c in range(chunks):
        own_copy(c).start()
    lax.fori_loop(1, n, greet, 0)
    for side in range(2):
        @pl.when(has[side])
        def _(side=side):
            pl.semaphore_signal(
                barrier, inc=1, device_id={"az": az + (2 * side - 1)}, device_id_type=MESH
            )
    pl.semaphore_wait(barrier, n - 1 + jnp.minimum(az, 1) + jnp.minimum(az_count - 1 - az, 1))

    def send_tab(k, carry):
        tab_copy(k).start()
        return carry
    lax.fori_loop(1, n, send_tab, 0)
    for c in range(chunks):
        def send(k, carry, c=c):
            strip_copy(c, k).start()
            return carry
        lax.fori_loop(1, n, send, 0)
    loads = [
        pltpu.make_async_copy(source, target, table_sem.at[i])
        for i, (source, target) in enumerate(zip((table_hbm, *tables_hbm), (table, *tables)))
    ]
    for load in loads:
        load.start()

    lane_slot = lax.broadcasted_iota(jnp.int32, (step, 128), 1) // looks
    first_line = az * lines
    gathered[me] = mine[...]

    def tab_arrive(k, carry):
        tab_copy(k).wait_recv()
        return carry
    lax.fori_loop(1, n, tab_arrive, 0)
    to_scalars = pltpu.make_async_copy(gathered, tab, table_sem.at[6])
    to_scalars.start()
    to_scalars.wait()
    for load in loads:
        load.wait()
    every_slot = table[0]
    for j in range(1, slots):
        every_slot = every_slot + table[j]

    def slot_of(row):
        return lax.rem(me - row + n, n)

    for c in range(chunks):
        own_copy(c).wait()

        def arrive(k, carry, c=c):
            strip_copy(c, k).wait_recv()
            return carry
        lax.fori_loop(1, n, arrive, 0)
        line = first_line + c * step + lax.broadcasted_iota(jnp.int32, (step, 128), 0)

        def powers(k, carry, c=c):
            re = strips[c][k, 0].astype(jnp.float32)
            im = strips[c][k, 1].astype(jnp.float32)
            power[k] = split_dot(re * re + im * im, every_slot)
            return carry
        lax.fori_loop(0, n, powers, 0)

        def pairs_of(k, carry, c=c, line=line):
            row = peer(k)
            at = slot_of(row)
            ref_re = strips[c][at, 0].astype(jnp.float32)
            ref_im = strips[c][at, 1].astype(jnp.float32)
            sum_re = jnp.zeros((step, 128), jnp.float32)
            sum_im = jnp.zeros((step, 128), jnp.float32)
            sec_power = jnp.zeros((step, 128), jnp.float32)
            alive = jnp.zeros((step, 128), jnp.float32)
            for j in range(slots):
                other = slot_of(tab[tab[row, 1, j], 4, 0])
                sec_re = strips[c][other, 0].astype(jnp.float32)
                sec_im = strips[c][other, 1].astype(jnp.float32)
                sum_re = sum_re + split_dot(ref_re * sec_re + ref_im * sec_im, table[j])
                sum_im = sum_im + split_dot(ref_im * sec_re - ref_re * sec_im, table[j])
                own_lanes = lane_slot == j
                sec_power = jnp.where(own_lanes, power[other], sec_power)
                alive = jnp.where(
                    own_lanes & (line >= tab[row, 2, j]) & (line < tab[row, 3, j]), 1.0, alive
                )

            def multilook(values):
                return jnp.sum((values * alive).reshape(rows, LA, 128), axis=1) / (LA * LR)

            look_re = multilook(sum_re)
            look_im = multilook(sum_im)
            denominator = jnp.maximum(jnp.sqrt(multilook(power[at]) * multilook(sec_power)), 0.5)
            coherent_re = look_re / denominator
            coherent_im = look_im / denominator
            ready[k, 0, pl.ds(c * rows, rows)] = coherent_re
            ready[k, 1, pl.ds(c * rows, rows)] = coherent_im
            ready[k, 2, pl.ds(c * rows, rows)] = jnp.sqrt(
                coherent_re * coherent_re + coherent_im * coherent_im
            )
            return carry

        def pairs_and_send(k, carry):
            pairs_of(k, carry)
            back_copy(k).start()
            return carry

        if c < chunks - 1:
            lax.fori_loop(0, n, pairs_of, 0)
        else:
            lax.fori_loop(1, n, pairs_and_send, 0)
            pairs_of(0, 0)

    def finish(k, carry):
        back_copy(k).wait_recv()
        return carry
    lax.fori_loop(1, n, finish, 0)

    lane = lax.broadcasted_iota(jnp.int32, (3, own, 128), 2) // looks
    total = [jnp.zeros((3, own, 128), jnp.float32) for _ in range(slots)]
    for d in range(n):
        piece = jnp.where(me == d, ready[0], landed[d])
        for j in range(slots):
            shift = ((d - j) * looks) % 128
            moved = pltpu.roll(piece, shift, 2) if shift else piece
            total[j] = jnp.where(lane == d, moved, total[j])
    for j in range(slots):
        cells[:, j] = total[j][:2]
    for side in range(2):
        @pl.when(has[side])
        def _(side=side):
            halo_copy(side).start()
    for j in range(slots):
        magnitude[j] = total[j][2]

    def drain(k, carry):
        for c in range(chunks):
            strip_copy(c, k).wait_send()
        back_copy(k).wait_send()
        tab_copy(k).wait_send()
        return carry
    lax.fori_loop(1, n, drain, 0)
    for side in range(2):
        @pl.when(has[1 - side])
        def _(side=side):
            halo_copy(side).wait_recv()

        @pl.when(jnp.logical_not(has[1 - side]))
        def _(side=side):
            halo[side] = jnp.zeros(halo.shape[1:], jnp.float32)
    goldstein(jnp.concatenate([halo[1], cells[...], halo[0]], axis=2), *tables, filtered)
    for side in range(2):
        @pl.when(has[side])
        def _(side=side):
            halo_copy(side).wait_send()


def whole_program(slc, pairs, position, ranges):
    n = lax.axis_size("acq")
    slots = pairs.shape[0]
    lines, samples = slc.shape[2:]
    width = samples // n
    chunks = 4
    own = lines // LA
    table = look_table(width, slots)
    tables = goldstein_tables(128)
    vmem = pl.BlockSpec(memory_space=pltpu.VMEM)
    hbm = pl.BlockSpec(memory_space=pltpu.HBM)
    dma = pltpu.SemaphoreType.DMA
    return pl.pallas_call(
        functools.partial(whole_kernel, n, slots, chunks),
        out_shape=(
            jax.ShapeDtypeStruct((2, slots, own, 128), jnp.float32),
            jax.ShapeDtypeStruct((slots, own, 128), jnp.float32),
        ),
        in_specs=[vmem] * 3 + [hbm] * (2 + len(tables)),
        out_specs=(vmem, vmem),
        scratch_shapes=[pltpu.VMEM((n, 2, lines // chunks, width), jnp.bfloat16)] * chunks
        + [pltpu.VMEM(t.shape, t.dtype) for t in (table, *tables)]
        + [
            pltpu.VMEM((8, 128), jnp.int32),
            pltpu.VMEM((n, 8, 128), jnp.int32),
            pltpu.SMEM((n, 8, 128), jnp.int32),
            pltpu.VMEM((n, lines // chunks, 128), jnp.float32),
            pltpu.VMEM((n, 3, own, 128), jnp.float32),
            pltpu.VMEM((n, 3, own, 128), jnp.float32),
            pltpu.VMEM((2, slots, own, 128), jnp.float32),
            pltpu.VMEM((2, 2, slots, HALF, 128), jnp.float32),
            dma((chunks,)),
            dma((chunks, n)),
            dma((chunks, n)),
            dma((n,)),
            dma((n,)),
            dma((n,)),
            dma((n,)),
            dma((7,)),
            dma((2,)),
            dma((2,)),
        ],
        compiler_params=pltpu.CompilerParams(
            collective_id=0, has_side_effects=True, vmem_limit_bytes=63 * 2**20
        ),
    )(pairs.T, position[:, None], ranges.T, slc, table, *tables)


def goldstein_tables(columns):
    ticks = np.arange(PATCH)
    angle = 2.0 * math.pi / PATCH * ((ticks[:, None] * ticks[None, :]) % PATCH)
    cos, sin = np.cos(angle), np.sin(angle)
    window = np.sin((ticks + 0.5) * (math.pi / PATCH)) ** 2
    left = np.block([[cos, sin], [-sin, cos]]) * np.tile(window, 2)[None, :]
    left_back = np.block([[cos, -sin], [sin, cos]]) / (PATCH * PATCH)
    eye = np.eye(columns // PATCH)
    wide_cos, wide_sin = np.kron(eye, cos), np.kron(eye, sin)
    wide_window = np.tile(window, columns // PATCH)
    forward, backward = [], []
    for offset in (0, HALF):
        keep = np.arange(columns) < (columns - PATCH if offset else columns)
        scale = (wide_window * keep)[:, None]
        into = [np.roll(scale * m, offset, axis=0) for m in (wide_cos, wide_sin)]
        forward.append(np.block([[into[0], -into[1]], [into[1], into[0]]]))
        back = [np.roll(m * keep[None, :], offset, axis=1) for m in (wide_cos, wide_sin)]
        backward.append(np.block([[back[0], back[1]], [-back[1], back[0]]]))
    ones = np.kron(eye, np.ones((PATCH, PATCH))) / (PATCH * PATCH)
    arrays = (left, left_back, np.concatenate(forward, 1), np.concatenate(backward, 0), ones)
    return tuple(jnp.asarray(a, jnp.float32) for a in arrays)


def goldstein(cells, left, left_back, forward, backward, ones, out):
    dot = functools.partial(
        jnp.dot, precision=lax.Precision.HIGHEST, preferred_element_type=jnp.float32
    )
    slots, extended, columns = cells.shape[1:]
    own = extended - 2 * HALF
    count = own // HALF + 1
    wide = dot(
        jnp.concatenate(
            [cells[0].reshape(slots * extended, columns), cells[1].reshape(slots * extended, columns)],
            axis=1,
        ),
        forward[...],
    )
    pieces = [(s, k, o) for s in range(slots) for k in range(count) for o in range(2)]

    def part(s, k, o, plane):
        row = s * extended + k * HALF
        col = (2 * o + plane) * columns
        return wide[row : row + PATCH, col : col + columns]

    stacked = jnp.concatenate(
        [jnp.concatenate([part(*p, 0) for p in pieces], axis=1),
         jnp.concatenate([part(*p, 1) for p in pieces], axis=1)],
        axis=0,
    )
    spectrum = dot(left[...], stacked)
    spec_re, spec_im = spectrum[:PATCH], spectrum[PATCH:]
    amplitude = jnp.sqrt(jnp.sqrt(spec_re * spec_re + spec_im * spec_im + 1e-06))
    sums = jnp.sum(amplitude, axis=0, keepdims=True)
    sums = jnp.concatenate(
        [sums[:, i * columns : (i + 1) * columns] for i in range(len(pieces))], axis=0
    )
    means = dot(sums, ones[...])
    means = jnp.concatenate([means[i : i + 1] for i in range(len(pieces))], axis=1)
    response = amplitude / means
    restored = dot(
        left_back[...], jnp.concatenate([response * spec_re, response * spec_im], axis=0)
    )

    def taken(s, k, o, plane, low):
        row = plane * PATCH + low
        col = pieces.index((s, k, o)) * columns
        return restored[row : row + HALF, col : col + columns]

    summed = jnp.concatenate(
        [
            jnp.concatenate(
                [
                    taken(s, r, o, plane, HALF) + taken(s, r + 1, o, plane, 0)
                    for o in range(2)
                    for plane in range(2)
                ],
                axis=1,
            )
            for s in range(slots)
            for r in range(own // HALF)
        ],
        axis=0,
    )
    result = dot(summed, backward[...])
    for plane in range(2):
        out[plane] = result[:, plane * columns : (plane + 1) * columns].reshape(slots, own, columns)


def solution(mesh):
    return jax.shard_map(
        whole_program,
        mesh=mesh,
        in_specs=(
            P(None, ("groups", "acq"), "az", None),
            P(("groups", "acq"), None),
            P(("groups", "acq")),
            P(("groups", "acq"), None),
        ),
        out_specs=(P(None, ("groups", "acq"), "az", None), P(("groups", "acq"), "az", None)),
        check_vma=False,
    )
```

```python
import functools
import math

import jax
import jax.numpy as jnp
import numpy as np
from jax import lax
from jax.experimental import pallas as pl
from jax.experimental.pallas import tpu as pltpu
from jax.sharding import PartitionSpec as P

LA = 8
LR = 32
PATCH = 32
HALF = PATCH // 2
MESH = pl.DeviceIdType.MESH


def look_table(width, slots):
    looks = width // LR
    table = np.zeros((width, 128), np.float32)
    for j in range(slots):
        table[np.arange(width), j * looks + np.arange(width) // LR] = 1.0
    return jnp.asarray(table, jnp.bfloat16)


def split_dot(values, table):
    high = values.astype(jnp.bfloat16)
    low = (values - high.astype(jnp.float32)).astype(jnp.bfloat16)
    both = jnp.dot(
        jnp.concatenate([high, low], axis=0), table, preferred_element_type=jnp.float32
    )
    return both[: values.shape[0]] + both[values.shape[0] :]


def whole_kernel(n, slots, chunks, pairs, position, ranges, x, table_hbm, *rest):
    tables_hbm, (filtered, magnitude), scratch = rest[:5], rest[5:7], rest[7:]
    strips, scratch = scratch[:chunks], scratch[chunks:]
    table, tables, scratch = scratch[0], scratch[1:6], scratch[6:]
    mine, gathered, tab, power, ready, landed, cells, halo, scratch = *scratch[:8], scratch[8:]
    own_sem, send_sem, recv_sem, back_send, back_recv, tab_send, tab_recv, table_sem, halo_send, halo_recv = scratch
    me = lax.axis_index("acq")
    az = lax.axis_index("az")
    az_count = lax.axis_size("az")
    lines = x.shape[2]
    width = x.shape[3] // n
    looks = width // LR
    step = lines // chunks
    rows = step // LA
    own = lines // LA
    barrier = pltpu.get_barrier_semaphore()

    def peer(k):
        return lax.rem(me + k, n)

    def greet(k, carry):
        pl.semaphore_signal(barrier, inc=1, device_id={"acq": peer(k)}, device_id_type=MESH)
        return carry

    def strip_copy(c, k):
        return pltpu.make_async_remote_copy(
            src_ref=x.at[:, 0, pl.ds(c * step, step), pl.ds(pl.multiple_of(peer(k) * width, 128), width)],
            dst_ref=strips[c].at[k],
            send_sem=send_sem.at[c, k],
            recv_sem=recv_sem.at[c, k],
            device_id={"acq": peer(k)},
            device_id_type=MESH,
        )

    def own_copy(c):
        return pltpu.make_async_copy(
            x.at[:, 0, pl.ds(c * step, step), pl.ds(pl.multiple_of(me * width, 128), width)],
            strips[c].at[0],
            own_sem.at[c],
        )

    def tab_copy(k):
        return pltpu.make_async_remote_copy(
            src_ref=mine,
            dst_ref=gathered.at[me],
            send_sem=tab_send.at[k],
            recv_sem=tab_recv.at[k],
            device_id={"acq": peer(k)},
            device_id_type=MESH,
        )

    def back_copy(k):
        return pltpu.make_async_remote_copy(
            src_ref=ready.at[k],
            dst_ref=landed.at[me],
            send_sem=back_send.at[k],
            recv_sem=back_recv.at[k],
            device_id={"acq": peer(k)},
            device_id_type=MESH,
        )

    def halo_copy(side):
        return pltpu.make_async_remote_copy(
            src_ref=cells.at[:, :, pl.ds(0 if side == 0 else own - HALF, HALF)],
            dst_ref=halo.at[side],
            send_sem=halo_send.at[side],
            recv_sem=halo_recv.at[side],
            device_id={"az": az + (2 * side - 1)},
            device_id_type=MESH,
        )

    has = (az > 0, az < az_count - 1)
    mine[...] = jnp.zeros_like(mine)
    mine[0:2, 0:slots] = pairs[...]
    mine[2:4, 0:slots] = ranges[...]
    mine[4:5, 0:1] = position[...]
    for c in range(chunks):
        own_copy(c).start()
    lax.fori_loop(1, n, greet, 0)
    for side in range(2):
        @pl.when(has[side])
        def _(side=side):
            pl.semaphore_signal(
                barrier, inc=1, device_id={"az": az + (2 * side - 1)}, device_id_type=MESH
            )
    pl.semaphore_wait(barrier, n - 1 + jnp.minimum(az, 1) + jnp.minimum(az_count - 1 - az, 1))

    def send_tab(k, carry):
        tab_copy(k).start()
        return carry
    lax.fori_loop(1, n, send_tab, 0)
    for c in range(chunks):
        def send(i, carry, c=c):
            strip_copy(c, 1 + lax.rem(i + n // 2 - 1, n - 1)).start()
            return carry
        lax.fori_loop(0, n - 1, send, 0)
    loads = [
        pltpu.make_async_copy(source, target, table_sem.at[i])
        for i, (source, target) in enumerate(zip((table_hbm, *tables_hbm), (table, *tables)))
    ]
    for load in loads:
        load.start()

    lane_slot = lax.broadcasted_iota(jnp.int32, (step, 128), 1) // looks
    first_line = az * lines
    gathered[me] = mine[...]

    def tab_arrive(k, carry):
        tab_copy(k).wait_recv()
        return carry
    lax.fori_loop(1, n, tab_arrive, 0)
    to_scalars = pltpu.make_async_copy(gathered, tab, table_sem.at[6])
    to_scalars.start()
    to_scalars.wait()
    for load in loads:
        load.wait()
    def slot_of(row):
        return lax.rem(me - row + n, n)

    for c in range(chunks):
        own_copy(c).wait()

        def arrive(k, carry, c=c):
            strip_copy(c, k).wait_recv()
            return carry
        lax.fori_loop(1, n, arrive, 0)
        line = first_line + c * step + lax.broadcasted_iota(jnp.int32, (step, 128), 0)

        def powers(k, carry, c=c):
            re = strips[c][k, 0].astype(jnp.float32)
            im = strips[c][k, 1].astype(jnp.float32)
            power[k] = split_dot(re * re + im * im, table[...])
            return carry
        lax.fori_loop(0, n, powers, 0)

        def pairs_of(k, carry, c=c, line=line):
            row = peer(k)
            at = slot_of(row)
            ref_re = strips[c][at, 0].astype(jnp.float32)
            ref_im = strips[c][at, 1].astype(jnp.float32)
            sum_re = jnp.zeros((step, 128), jnp.float32)
            sum_im = jnp.zeros((step, 128), jnp.float32)
            sec_power = jnp.zeros((step, 128), jnp.float32)
            alive = jnp.zeros((step, 128), jnp.float32)
            products = []
            for j in range(slots):
                other = slot_of(tab[tab[row, 1, j], 4, 0])
                sec_re = strips[c][other, 0].astype(jnp.float32)
                sec_im = strips[c][other, 1].astype(jnp.float32)
                products.append(ref_re * sec_re + ref_im * sec_im)
                products.append(ref_im * sec_re - ref_re * sec_im)
                own_lanes = lane_slot == j
                sec_power = jnp.where(own_lanes, power[other], sec_power)
                alive = jnp.where(
                    own_lanes & (line >= tab[row, 2, j]) & (line < tab[row, 3, j]), 1.0, alive
                )
            sums = split_dot(jnp.concatenate(products, axis=0), table[...])
            for j in range(slots):
                own_lanes = lane_slot == j
                at_re = 2 * j * step
                sum_re = jnp.where(own_lanes, sums[at_re : at_re + step], sum_re)
                sum_im = jnp.where(own_lanes, sums[at_re + step : at_re + 2 * step], sum_im)

            def multilook(values):
                return jnp.sum((values * alive).reshape(rows, LA, 128), axis=1) / (LA * LR)

            look_re = multilook(sum_re)
            look_im = multilook(sum_im)
            denominator = jnp.maximum(jnp.sqrt(multilook(power[at]) * multilook(sec_power)), 0.5)
            coherent_re = look_re / denominator
            coherent_im = look_im / denominator
            ready[k, 0, pl.ds(c * rows, rows)] = coherent_re
            ready[k, 1, pl.ds(c * rows, rows)] = coherent_im
            ready[k, 2, pl.ds(c * rows, rows)] = jnp.sqrt(
                coherent_re * coherent_re + coherent_im * coherent_im
            )
            return carry

        def pairs_and_send(k, carry):
            pairs_of(k, carry)
            back_copy(k).start()
            return carry

        if c < chunks - 1:
            lax.fori_loop(0, n, pairs_of, 0)
        else:
            lax.fori_loop(1, n, pairs_and_send, 0)
            pairs_of(0, 0)

    def finish(k, carry):
        back_copy(k).wait_recv()
        return carry
    lax.fori_loop(1, n, finish, 0)

    lane = lax.broadcasted_iota(jnp.int32, (3, own, 128), 2) // looks
    total = [jnp.zeros((3, own, 128), jnp.float32) for _ in range(slots)]
    for d in range(n):
        piece = jnp.where(me == d, ready[0], landed[d])
        for j in range(slots):
            shift = ((d - j) * looks) % 128
            moved = pltpu.roll(piece, shift, 2) if shift else piece
            total[j] = jnp.where(lane == d, moved, total[j])
    for j in range(slots):
        cells[:, j] = total[j][:2]
    for side in range(2):
        @pl.when(has[side])
        def _(side=side):
            halo_copy(side).start()
    for j in range(slots):
        magnitude[j] = total[j][2]

    def drain(k, carry):
        for c in range(chunks):
            strip_copy(c, k).wait_send()
        back_copy(k).wait_send()
        tab_copy(k).wait_send()
        return carry
    lax.fori_loop(1, n, drain, 0)
    for side in range(2):
        @pl.when(has[1 - side])
        def _(side=side):
            halo_copy(side).wait_recv()

        @pl.when(jnp.logical_not(has[1 - side]))
        def _(side=side):
            halo[side] = jnp.zeros(halo.shape[1:], jnp.float32)
    goldstein(jnp.concatenate([halo[1], cells[...], halo[0]], axis=2), *tables, filtered)
    for side in range(2):
        @pl.when(has[side])
        def _(side=side):
            halo_copy(side).wait_send()


def whole_program(slc, pairs, position, ranges):
    n = lax.axis_size("acq")
    slots = pairs.shape[0]
    lines, samples = slc.shape[2:]
    width = samples // n
    chunks = 4
    own = lines // LA
    table = look_table(width, slots)
    tables = goldstein_tables(128)
    vmem = pl.BlockSpec(memory_space=pltpu.VMEM)
    hbm = pl.BlockSpec(memory_space=pltpu.HBM)
    dma = pltpu.SemaphoreType.DMA
    return pl.pallas_call(
        functools.partial(whole_kernel, n, slots, chunks),
        out_shape=(
            jax.ShapeDtypeStruct((2, slots, own, 128), jnp.float32),
            jax.ShapeDtypeStruct((slots, own, 128), jnp.float32),
        ),
        in_specs=[vmem] * 3 + [hbm] * (2 + len(tables)),
        out_specs=(vmem, vmem),
        scratch_shapes=[pltpu.VMEM((n, 2, lines // chunks, width), jnp.bfloat16)] * chunks
        + [pltpu.VMEM(t.shape, t.dtype) for t in (table, *tables)]
        + [
            pltpu.VMEM((8, 128), jnp.int32),
            pltpu.VMEM((n, 8, 128), jnp.int32),
            pltpu.SMEM((n, 8, 128), jnp.int32),
            pltpu.VMEM((n, lines // chunks, 128), jnp.float32),
            pltpu.VMEM((n, 3, own, 128), jnp.float32),
            pltpu.VMEM((n, 3, own, 128), jnp.float32),
            pltpu.VMEM((2, slots, own, 128), jnp.float32),
            pltpu.VMEM((2, 2, slots, HALF, 128), jnp.float32),
            dma((chunks,)),
            dma((chunks, n)),
            dma((chunks, n)),
            dma((n,)),
            dma((n,)),
            dma((n,)),
            dma((n,)),
            dma((7,)),
            dma((2,)),
            dma((2,)),
        ],
        compiler_params=pltpu.CompilerParams(
            collective_id=0, has_side_effects=True, vmem_limit_bytes=63 * 2**20
        ),
    )(pairs.T, position[:, None], ranges.T, slc, table, *tables)


def goldstein_tables(columns):
    ticks = np.arange(PATCH)
    angle = 2.0 * math.pi / PATCH * ((ticks[:, None] * ticks[None, :]) % PATCH)
    cos, sin = np.cos(angle), np.sin(angle)
    window = np.sin((ticks + 0.5) * (math.pi / PATCH)) ** 2
    left = np.block([[cos, sin], [-sin, cos]]) * np.tile(window, 2)[None, :]
    left_back = np.block([[cos, -sin], [sin, cos]]) / (PATCH * PATCH)
    eye = np.eye(columns // PATCH)
    wide_cos, wide_sin = np.kron(eye, cos), np.kron(eye, sin)
    wide_window = np.tile(window, columns // PATCH)
    forward, backward = [], []
    for offset in (0, HALF):
        keep = np.arange(columns) < (columns - PATCH if offset else columns)
        scale = (wide_window * keep)[:, None]
        into = [np.roll(scale * m, offset, axis=0) for m in (wide_cos, wide_sin)]
        forward.append(np.block([[into[0], -into[1]], [into[1], into[0]]]))
        back = [np.roll(m * keep[None, :], offset, axis=1) for m in (wide_cos, wide_sin)]
        backward.append(np.block([[back[0], back[1]], [-back[1], back[0]]]))
    ones = np.kron(eye, np.ones((PATCH, PATCH))) / (PATCH * PATCH)
    arrays = (left, left_back, np.concatenate(forward, 1), np.concatenate(backward, 0), ones)
    return tuple(jnp.asarray(a, jnp.float32) for a in arrays)


def goldstein(cells, left, left_back, forward, backward, ones, out):
    dot = functools.partial(
        jnp.dot, precision=lax.Precision.HIGHEST, preferred_element_type=jnp.float32
    )
    slots, extended, columns = cells.shape[1:]
    own = extended - 2 * HALF
    count = own // HALF + 1
    wide = dot(
        jnp.concatenate(
            [cells[0].reshape(slots * extended, columns), cells[1].reshape(slots * extended, columns)],
            axis=1,
        ),
        forward[...],
    )
    pieces = [(s, k, o) for s in range(slots) for k in range(count) for o in range(2)]

    def part(s, k, o, plane):
        row = s * extended + k * HALF
        col = (2 * o + plane) * columns
        return wide[row : row + PATCH, col : col + columns]

    stacked = jnp.concatenate(
        [jnp.concatenate([part(*p, 0) for p in pieces], axis=1),
         jnp.concatenate([part(*p, 1) for p in pieces], axis=1)],
        axis=0,
    )
    spectrum = dot(left[...], stacked)
    spec_re, spec_im = spectrum[:PATCH], spectrum[PATCH:]
    amplitude = jnp.sqrt(jnp.sqrt(spec_re * spec_re + spec_im * spec_im + 1e-06))
    sums = jnp.sum(amplitude, axis=0, keepdims=True)
    sums = jnp.concatenate(
        [sums[:, i * columns : (i + 1) * columns] for i in range(len(pieces))], axis=0
    )
    means = dot(sums, ones[...])
    means = jnp.concatenate([means[i : i + 1] for i in range(len(pieces))], axis=1)
    response = amplitude / means
    restored = dot(
        left_back[...], jnp.concatenate([response * spec_re, response * spec_im], axis=0)
    )

    def taken(s, k, o, plane, low):
        row = plane * PATCH + low
        col = pieces.index((s, k, o)) * columns
        return restored[row : row + HALF, col : col + columns]

    summed = jnp.concatenate(
        [
            jnp.concatenate(
                [
                    taken(s, r, o, plane, HALF) + taken(s, r + 1, o, plane, 0)
                    for o in range(2)
                    for plane in range(2)
                ],
                axis=1,
            )
            for s in range(slots)
            for r in range(own // HALF)
        ],
        axis=0,
    )
    result = dot(summed, backward[...])
    for plane in range(2):
        out[plane] = result[:, plane * columns : (plane + 1) * columns].reshape(slots, own, columns)


def solution(mesh):
    return jax.shard_map(
        whole_program,
        mesh=mesh,
        in_specs=(
            P(None, ("groups", "acq"), "az", None),
            P(("groups", "acq"), None),
            P(("groups", "acq")),
            P(("groups", "acq"), None),
        ),
        out_specs=(P(None, ("groups", "acq"), "az", None), P(("groups", "acq"), "az", None)),
        check_vma=False,
    )
```

```python
import functools
import math

import jax
import jax.numpy as jnp
import numpy as np
from jax import lax
from jax.experimental import pallas as pl
from jax.experimental.pallas import tpu as pltpu
from jax.sharding import PartitionSpec as P

LA = 8
LR = 32
PATCH = 32
HALF = PATCH // 2
MESH = pl.DeviceIdType.MESH


def look_table(width, slots):
    looks = width // LR
    table = np.zeros((width, 128), np.float32)
    for j in range(slots):
        table[np.arange(width), j * looks + np.arange(width) // LR] = 1.0
    return jnp.asarray(table, jnp.bfloat16)


def split_dot(values, table):
    high = values.astype(jnp.bfloat16)
    low = (values - high.astype(jnp.float32)).astype(jnp.bfloat16)
    both = jnp.dot(
        jnp.concatenate([high, low], axis=0), table, preferred_element_type=jnp.float32
    )
    return both[: values.shape[0]] + both[values.shape[0] :]


def whole_kernel(n, slots, chunks, pairs, position, ranges, x, table_hbm, *rest):
    tables_hbm, out, scratch = rest[:5], rest[5], rest[6:]
    strips, scratch = scratch[:chunks], scratch[chunks:]
    table, tables, scratch = scratch[0], scratch[1:6], scratch[6:]
    mine, gathered, tab, power, ready, landed, cells, halo, scratch = *scratch[:8], scratch[8:]
    own_sem, send_sem, recv_sem, back_send, back_recv, tab_send, tab_recv, table_sem, halo_send, halo_recv = scratch
    me = lax.axis_index("acq")
    az = lax.axis_index("az")
    az_count = lax.axis_size("az")
    lines = x.shape[2]
    width = x.shape[3] // n
    looks = width // LR
    step = lines // chunks
    rows = step // LA
    own = lines // LA
    barrier = pltpu.get_barrier_semaphore()

    def peer(k):
        return lax.rem(me + k, n)

    def greet(k, carry):
        pl.semaphore_signal(barrier, inc=1, device_id={"acq": peer(k)}, device_id_type=MESH)
        return carry

    def strip_copy(c, k):
        return pltpu.make_async_remote_copy(
            src_ref=x.at[:, 0, pl.ds(c * step, step), pl.ds(pl.multiple_of(peer(k) * width, 128), width)],
            dst_ref=strips[c].at[k],
            send_sem=send_sem.at[c, k],
            recv_sem=recv_sem.at[c, k],
            device_id={"acq": peer(k)},
            device_id_type=MESH,
        )

    def own_copy(c):
        return pltpu.make_async_copy(
            x.at[:, 0, pl.ds(c * step, step), pl.ds(pl.multiple_of(me * width, 128), width)],
            strips[c].at[0],
            own_sem.at[c],
        )

    def tab_copy(k):
        return pltpu.make_async_remote_copy(
            src_ref=mine,
            dst_ref=gathered.at[me],
            send_sem=tab_send.at[k],
            recv_sem=tab_recv.at[k],
            device_id={"acq": peer(k)},
            device_id_type=MESH,
        )

    def back_copy(k):
        return pltpu.make_async_remote_copy(
            src_ref=ready.at[k],
            dst_ref=landed.at[me],
            send_sem=back_send.at[k],
            recv_sem=back_recv.at[k],
            device_id={"acq": peer(k)},
            device_id_type=MESH,
        )

    def halo_copy(side):
        return pltpu.make_async_remote_copy(
            src_ref=cells.at[:, :, pl.ds(0 if side == 0 else own - HALF, HALF)],
            dst_ref=halo.at[side],
            send_sem=halo_send.at[side],
            recv_sem=halo_recv.at[side],
            device_id={"az": az + (2 * side - 1)},
            device_id_type=MESH,
        )

    has = (az > 0, az < az_count - 1)
    lax.fori_loop(1, n, greet, 0)
    for side in range(2):
        @pl.when(has[side])
        def _(side=side):
            pl.semaphore_signal(
                barrier, inc=1, device_id={"az": az + (2 * side - 1)}, device_id_type=MESH
            )
    mine[...] = jnp.zeros_like(mine)
    mine[0:2, 0:slots] = pairs[...]
    mine[2:4, 0:slots] = ranges[...]
    mine[4:5, 0:1] = position[...]
    for c in range(chunks):
        own_copy(c).start()
    pl.semaphore_wait(barrier, n - 1 + jnp.minimum(az, 1) + jnp.minimum(az_count - 1 - az, 1))

    def send_tab(k, carry):
        tab_copy(k).start()
        return carry
    lax.fori_loop(1, n, send_tab, 0)
    for c in range(chunks):
        def send(i, carry, c=c):
            strip_copy(c, 1 + lax.rem(i + n // 2 - 1, n - 1)).start()
            return carry
        lax.fori_loop(0, n - 1, send, 0)
    loads = [
        pltpu.make_async_copy(source, target, table_sem.at[i])
        for i, (source, target) in enumerate(zip((table_hbm, *tables_hbm), (table, *tables)))
    ]
    for load in loads:
        load.start()

    lane_slot = lax.broadcasted_iota(jnp.int32, (step, 128), 1) // looks
    first_line = az * lines
    gathered[me] = mine[...]

    def tab_arrive(k, carry):
        tab_copy(k).wait_recv()
        return carry
    lax.fori_loop(1, n, tab_arrive, 0)
    to_scalars = pltpu.make_async_copy(gathered, tab, table_sem.at[6])
    to_scalars.start()
    to_scalars.wait()
    for load in loads:
        load.wait()
    def slot_of(row):
        return lax.rem(me - row + n, n)

    for c in range(chunks):
        own_copy(c).wait()

        def arrive(k, carry, c=c):
            strip_copy(c, k).wait_recv()
            return carry
        lax.fori_loop(1, n, arrive, 0)
        line = first_line + c * step + lax.broadcasted_iota(jnp.int32, (step, 128), 0)

        def powers(k, carry, c=c):
            re = strips[c][k, 0].astype(jnp.float32)
            im = strips[c][k, 1].astype(jnp.float32)
            power[k] = split_dot(re * re + im * im, table[...])
            return carry
        lax.fori_loop(0, n, powers, 0)

        def pairs_of(k, carry, c=c, line=line):
            row = peer(k)
            at = slot_of(row)
            ref_re = strips[c][at, 0].astype(jnp.float32)
            ref_im = strips[c][at, 1].astype(jnp.float32)
            sum_re = jnp.zeros((step, 128), jnp.float32)
            sum_im = jnp.zeros((step, 128), jnp.float32)
            sec_power = jnp.zeros((step, 128), jnp.float32)
            alive = jnp.zeros((step, 128), jnp.float32)
            products = []
            for j in range(slots):
                other = slot_of(tab[tab[row, 1, j], 4, 0])
                sec_re = strips[c][other, 0].astype(jnp.float32)
                sec_im = strips[c][other, 1].astype(jnp.float32)
                products.append(ref_re * sec_re + ref_im * sec_im)
                products.append(ref_im * sec_re - ref_re * sec_im)
                own_lanes = lane_slot == j
                sec_power = jnp.where(own_lanes, power[other], sec_power)
                alive = jnp.where(
                    own_lanes & (line >= tab[row, 2, j]) & (line < tab[row, 3, j]), 1.0, alive
                )
            sums = split_dot(jnp.concatenate(products, axis=0), table[...])
            for j in range(slots):
                own_lanes = lane_slot == j
                at_re = 2 * j * step
                sum_re = jnp.where(own_lanes, sums[at_re : at_re + step], sum_re)
                sum_im = jnp.where(own_lanes, sums[at_re + step : at_re + 2 * step], sum_im)

            def multilook(values):
                return jnp.sum((values * alive).reshape(rows, LA, 128), axis=1) / (LA * LR)

            look_re = multilook(sum_re)
            look_im = multilook(sum_im)
            denominator = jnp.maximum(jnp.sqrt(multilook(power[at]) * multilook(sec_power)), 0.5)
            coherent_re = look_re / denominator
            coherent_im = look_im / denominator
            ready[k, 0, pl.ds(c * rows, rows)] = coherent_re
            ready[k, 1, pl.ds(c * rows, rows)] = coherent_im
            ready[k, 2, pl.ds(c * rows, rows)] = jnp.sqrt(
                coherent_re * coherent_re + coherent_im * coherent_im
            )
            return carry

        def pairs_and_send(k, carry):
            pairs_of(k, carry)
            back_copy(k).start()
            return carry

        if c < chunks - 1:
            lax.fori_loop(0, n, pairs_of, 0)
        else:
            lax.fori_loop(1, n, pairs_and_send, 0)
            pairs_of(0, 0)

    def finish(k, carry):
        back_copy(k).wait_recv()
        return carry
    lax.fori_loop(1, n, finish, 0)

    lane = lax.broadcasted_iota(jnp.int32, (3, own, 128), 2) // looks
    total = [jnp.zeros((3, own, 128), jnp.float32) for _ in range(slots)]
    for d in range(n):
        piece = jnp.where(me == d, ready[0], landed[d])
        for j in range(slots):
            shift = ((d - j) * looks) % 128
            moved = pltpu.roll(piece, shift, 2) if shift else piece
            total[j] = jnp.where(lane == d, moved, total[j])
    for j in range(slots):
        cells[:, j] = total[j][:2]
    for side in range(2):
        @pl.when(has[side])
        def _(side=side):
            halo_copy(side).start()
    for j in range(slots):
        out[2, j] = total[j][2]

    def drain(k, carry):
        for c in range(chunks):
            strip_copy(c, k).wait_send()
        back_copy(k).wait_send()
        tab_copy(k).wait_send()
        return carry
    lax.fori_loop(1, n, drain, 0)
    for side in range(2):
        @pl.when(has[1 - side])
        def _(side=side):
            halo_copy(side).wait_recv()

        @pl.when(jnp.logical_not(has[1 - side]))
        def _(side=side):
            halo[side] = jnp.zeros(halo.shape[1:], jnp.float32)
    goldstein(jnp.concatenate([halo[1], cells[...], halo[0]], axis=2), *tables, out)
    for side in range(2):
        @pl.when(has[side])
        def _(side=side):
            halo_copy(side).wait_send()


def whole_program(slc, pairs, position, ranges):
    n = lax.axis_size("acq")
    slots = pairs.shape[0]
    lines, samples = slc.shape[2:]
    width = samples // n
    chunks = 4
    own = lines // LA
    table = look_table(width, slots)
    tables = goldstein_tables(128)
    vmem = pl.BlockSpec(memory_space=pltpu.VMEM)
    hbm = pl.BlockSpec(memory_space=pltpu.HBM)
    dma = pltpu.SemaphoreType.DMA
    planes = pl.pallas_call(
        functools.partial(whole_kernel, n, slots, chunks),
        out_shape=jax.ShapeDtypeStruct((3, slots, own, 128), jnp.float32),
        in_specs=[vmem] * 3 + [hbm] * (2 + len(tables)),
        out_specs=vmem,
        scratch_shapes=[pltpu.VMEM((n, 2, lines // chunks, width), jnp.bfloat16)] * chunks
        + [pltpu.VMEM(t.shape, t.dtype) for t in (table, *tables)]
        + [
            pltpu.VMEM((8, 128), jnp.int32),
            pltpu.VMEM((n, 8, 128), jnp.int32),
            pltpu.SMEM((n, 8, 128), jnp.int32),
            pltpu.VMEM((n, lines // chunks, 128), jnp.float32),
            pltpu.VMEM((n, 3, own, 128), jnp.float32),
            pltpu.VMEM((n, 3, own, 128), jnp.float32),
            pltpu.VMEM((2, slots, own, 128), jnp.float32),
            pltpu.VMEM((2, 2, slots, HALF, 128), jnp.float32),
            dma((chunks,)),
            dma((chunks, n)),
            dma((chunks, n)),
            dma((n,)),
            dma((n,)),
            dma((n,)),
            dma((n,)),
            dma((7,)),
            dma((2,)),
            dma((2,)),
        ],
        compiler_params=pltpu.CompilerParams(
            collective_id=0, has_side_effects=True, vmem_limit_bytes=63 * 2**20
        ),
    )(pairs.T, position[:, None], ranges.T, slc, table, *tables)
    return (planes[:2], planes[2])


def goldstein_tables(columns):
    ticks = np.arange(PATCH)
    angle = 2.0 * math.pi / PATCH * ((ticks[:, None] * ticks[None, :]) % PATCH)
    cos, sin = np.cos(angle), np.sin(angle)
    window = np.sin((ticks + 0.5) * (math.pi / PATCH)) ** 2
    left = np.block([[cos, sin], [-sin, cos]]) * np.tile(window, 2)[None, :]
    left_back = np.block([[cos, -sin], [sin, cos]]) / (PATCH * PATCH)
    eye = np.eye(columns // PATCH)
    wide_cos, wide_sin = np.kron(eye, cos), np.kron(eye, sin)
    wide_window = np.tile(window, columns // PATCH)
    forward, backward = [], []
    for offset in (0, HALF):
        keep = np.arange(columns) < (columns - PATCH if offset else columns)
        scale = (wide_window * keep)[:, None]
        into = [np.roll(scale * m, offset, axis=0) for m in (wide_cos, wide_sin)]
        forward.append(np.block([[into[0], -into[1]], [into[1], into[0]]]))
        back = [np.roll(m * keep[None, :], offset, axis=1) for m in (wide_cos, wide_sin)]
        backward.append(np.block([[back[0], back[1]], [-back[1], back[0]]]))
    ones = np.kron(eye, np.ones((PATCH, PATCH))) / (PATCH * PATCH)
    arrays = (left, left_back, np.concatenate(forward, 1), np.concatenate(backward, 0), ones)
    return tuple(jnp.asarray(a, jnp.float32) for a in arrays)


def goldstein(cells, left, left_back, forward, backward, ones, out):
    dot = functools.partial(
        jnp.dot, precision=lax.Precision.HIGHEST, preferred_element_type=jnp.float32
    )
    slots, extended, columns = cells.shape[1:]
    own = extended - 2 * HALF
    count = own // HALF + 1
    wide = dot(
        jnp.concatenate(
            [cells[0].reshape(slots * extended, columns), cells[1].reshape(slots * extended, columns)],
            axis=1,
        ),
        forward[...],
    )
    pieces = [(s, k, o) for s in range(slots) for k in range(count) for o in range(2)]

    def part(s, k, o, plane):
        row = s * extended + k * HALF
        col = (2 * o + plane) * columns
        return wide[row : row + PATCH, col : col + columns]

    stacked = jnp.concatenate(
        [jnp.concatenate([part(*p, 0) for p in pieces], axis=1),
         jnp.concatenate([part(*p, 1) for p in pieces], axis=1)],
        axis=0,
    )
    spectrum = dot(left[...], stacked)
    spec_re, spec_im = spectrum[:PATCH], spectrum[PATCH:]
    amplitude = jnp.sqrt(jnp.sqrt(spec_re * spec_re + spec_im * spec_im + 1e-06))
    sums = jnp.sum(amplitude, axis=0, keepdims=True)
    sums = jnp.concatenate(
        [sums[:, i * columns : (i + 1) * columns] for i in range(len(pieces))], axis=0
    )
    means = dot(sums, ones[...])
    means = jnp.concatenate([means[i : i + 1] for i in range(len(pieces))], axis=1)
    response = amplitude / means
    restored = dot(
        left_back[...], jnp.concatenate([response * spec_re, response * spec_im], axis=0)
    )

    def taken(s, k, o, plane, low):
        row = plane * PATCH + low
        col = pieces.index((s, k, o)) * columns
        return restored[row : row + HALF, col : col + columns]

    summed = jnp.concatenate(
        [
            jnp.concatenate(
                [
                    taken(s, r, o, plane, HALF) + taken(s, r + 1, o, plane, 0)
                    for o in range(2)
                    for plane in range(2)
                ],
                axis=1,
            )
            for s in range(slots)
            for r in range(own // HALF)
        ],
        axis=0,
    )
    result = dot(summed, backward[...])
    for plane in range(2):
        out[plane] = result[:, plane * columns : (plane + 1) * columns].reshape(slots, own, columns)


def solution(mesh):
    return jax.shard_map(
        whole_program,
        mesh=mesh,
        in_specs=(
            P(None, ("groups", "acq"), "az", None),
            P(("groups", "acq"), None),
            P(("groups", "acq")),
            P(("groups", "acq"), None),
        ),
        out_specs=(P(None, ("groups", "acq"), "az", None), P(("groups", "acq"), "az", None)),
        check_vma=False,
    )
```
